256 devices in a mesh: tp: 8 (over z_lo, x), ep: 32 (over y, z_hi, core).
Axes of the slice: x: 4, y: 4, z: 8 (z_hi: 4, z_lo: 2; z = z_hi * 2 + z_lo), core: 2. Of those that a mesh axis runs over, the one named last changes fastest.
Arguments:
- tokens: bfloat16 [6144, 4096], P('ep', 'tp'), may hold values from -6 to 6
- routes: int32 [6144, 2], P('ep'), may hold values from 0 to 31, all different within a row; in each aligned block of 192 rows (0 to 191, 192 to 383, ...) at most 24 rows name the same one
- combine: float32 [6144, 2], P('ep'), may hold values from 0.2 to 1
- expert_slot: int32 [32], replicated, may hold values from 0 to 31, each once
- dense_gate: bfloat16 [4096, 3072], P('ep', 'tp'), may hold values from -0.09375 to 0.09375
- dense_up: bfloat16 [4096, 3072], P('ep', 'tp'), may hold values from -0.09375 to 0.09375
- dense_down: bfloat16 [3072, 4096], P('tp', 'ep'), may hold values from -0.109375 to 0.109375
- expert_gate: bfloat16 [32, 4096, 3072], P('ep', None, 'tp'), may hold values from -0.09375 to 0.09375
- expert_up: bfloat16 [32, 4096, 3072], P('ep', None, 'tp'), may hold values from -0.09375 to 0.09375
- expert_down: bfloat16 [32, 3072, 4096], P('ep', 'tp'), may hold values from -0.109375 to 0.109375
Outputs:
- mixed: bfloat16 [6144, 4096], P('ep', 'tp')
The draws below stay inside these ranges and needn't reach their ends.
Inputs may be any that keep to these rules, and one draw needn't show every extreme that they name: `routes`: the two experts of a row differ. In each aligned block of 192 rows no expert is named by more than 24 rows, and in every draw some expert is named by exactly 24 rows of some block. A permutation: expert e uses block expert_slot[e] of expert_gate, expert_up and expert_down.
All inputs are finite; a program needn't handle non-finite values.
Results may differ from the reference program's by a relative error of at most 0.015.
Values may be sent and summed in bfloat16 or wider, within the bound.
A program may use at most 128 MiB of HBM per device.

```python
import math
import jax
import jax.numpy as jnp
import numpy as np
from jax import lax

D = 4096
FF = 3072
FF_E = 3072
TOK_DEV = 192
EXPERTS = 32
TOKENS = 6144
CAP = 24
N_TP = 8
N_EP = 32


def levels(stream_key, dims, pieces, smallest, top_value):
    loudness, own = 1.0, jax.random.fold_in(stream_key, 6)
    for position, parts in pieces:
        draws = jnp.exp(jax.random.uniform(jax.random.fold_in(own, position), (parts,), jnp.float32, smallest / len(pieces), top_value / len(pieces)))
        loudness = loudness * jnp.repeat(draws, dims[position] // parts).reshape([-1 if axis == position else 1 for axis in range(len(dims))])
    return loudness


def assign_block(rng, own, number, rows, number_of, top, bound, skew):
    ranking = jax.random.permutation(rng, number_of)
    heavy_load, common = load_shares(number_of, rows * top, bound, skew, True), load_shares(number_of, rows * top, bound, skew, False)
    places = jnp.arange(number_of)

    def named(tallies, rotation):
        used = int((tallies > 0).sum())
        fixed = max(1, used // 4)
        shifted = fixed + (places - fixed + rotation * (used - fixed)) % max(1, number_of - fixed)
        return jnp.zeros((number_of,), jnp.int32).at[ranking[jnp.where(places < fixed, places, shifted)]].set(jnp.asarray(tallies, jnp.int32))

    tallies = jnp.where(number % 4 == 0, named(heavy_load, number // 4), named(common, number - number // 4 - 1))
    mixed = jax.random.permutation(jax.random.fold_in(own, 3), number_of)
    source_of, sink = mixed[0:number_of // 2 * 2:2], mixed[1:number_of // 2 * 2:2]
    room = jnp.minimum(tallies[source_of] - 1, bound - tallies[sink]) // 2
    room = jnp.where((source_of == ranking[0]) | (sink == ranking[0]) | (tallies[sink] == 0), 0, jnp.maximum(room, 0))
    shifted = jax.random.randint(jax.random.fold_in(own, 4), (number_of // 2,), 0, 1 << 20) % (room + 1)
    tallies = tallies.at[source_of].add(-shifted).at[sink].add(shifted)
    labels = jnp.searchsorted(jnp.cumsum(tallies), jnp.arange(rows * top), side="right").astype(jnp.int32)
    table = labels.reshape(top, rows).T
    table = table[jax.random.permutation(jax.random.fold_in(own, 1), rows)]
    rotation = jax.random.randint(jax.random.fold_in(own, 2), (rows, 1), 0, top)
    return jnp.take_along_axis(table, (jnp.arange(top)[None, :] + rotation) % top, axis=1)


def load_shares(amount, total, limit, slope, full):
    loads = [(1 << 20) // math.isqrt(grade ** slope) + 1 for grade in range(1, amount + 1)]
    largest = limit if full else min(limit, max(-(-total // amount), total * loads[0] // sum(loads)))
    least = 1 if total - largest >= amount - 1 else 0
    holding, rest = [largest] + [least] * (amount - 1), total - largest - least * (amount - 1)
    while rest > 0:
        movable = [i for i in range(1, amount) if holding[i] < largest] or [i for i in range(1, amount) if holding[i] < limit]
        pool, remaining = sum([loads[i] for i in movable]), rest
        for i in movable:
            addition = min(limit - holding[i], max(1, remaining * loads[i] // pool), rest)
            holding[i] = holding[i] + addition
            rest = rest - addition
    return np.array(holding)


def normal_values(stream_key, extent, spread, reach, pieces=(), kind=jnp.bfloat16):
    level = levels(stream_key, extent, pieces, -0.22, 0.18) if pieces else 1.0
    array = jax.random.normal(stream_key, extent, jnp.float32) * spread * level
    return jnp.minimum(jnp.maximum(array, -reach), reach).astype(kind)


def setup_inputs(seed: int = 0) -> dict:
    key_list = jax.random.split(jax.random.key(seed), 11)
    tokens = normal_values(key_list[0], (TOKENS, D), 1.0, 6.0, ((0, 32), (1, 8)))
    routes_keys = jax.random.split(jax.random.fold_in(key_list[1], 1), TOKENS // TOK_DEV)
    routes_turns = jax.random.permutation(jax.random.fold_in(key_list[1], 3), TOKENS // TOK_DEV)
    routes = jax.vmap(lambda own, number: assign_block(jax.random.fold_in(key_list[1], 2), own, number, TOK_DEV, EXPERTS, 2, CAP, 2))(routes_keys, routes_turns).reshape((TOKENS, 2))
    combine = jnp.clip(jnp.exp(math.log(1.0) - 1.609438 * jax.random.uniform(key_list[2], (TOKENS, 2), jnp.float32) ** levels(key_list[2], (TOKENS, 2), ((0, 32),), -0.2, 0.2)), 0.2, 1.0)
    expert_slot = jax.random.permutation(key_list[3], EXPERTS).astype(jnp.int32)
    dense_gate = normal_values(key_list[4], (D, FF), D ** -0.5, 0.09375, ((0, 32), (1, 8)))
    dense_up = normal_values(key_list[5], (D, FF), D ** -0.5, 0.09375, ((0, 32), (1, 8)))
    dense_down = normal_values(key_list[6], (FF, D), FF ** -0.5, 0.109375, ((0, 8), (1, 32)))
    expert_gate = normal_values(key_list[7], (EXPERTS, D, FF_E), D ** -0.5, 0.09375, ((0, 32), (2, 8)))
    expert_up = normal_values(key_list[8], (EXPERTS, D, FF_E), D ** -0.5, 0.09375, ((0, 32), (2, 8)))
    expert_down = normal_values(key_list[9], (EXPERTS, FF_E, D), FF_E ** -0.5, 0.109375, ((0, 32), (1, 8)))
    return dict(tokens=tokens, routes=routes, combine=combine, expert_slot=expert_slot, dense_gate=dense_gate, dense_up=dense_up, dense_down=dense_down, expert_gate=expert_gate, expert_up=expert_up, expert_down=expert_down)


def group_sum(hidden, down):
    width = hidden.shape[1] // N_TP

    def add(index, total):
        start = (index * width).astype(jnp.int32)
        part_h = lax.dynamic_slice_in_dim(hidden, start, width, 1)
        part_w = lax.dynamic_slice_in_dim(down, start, width, 0)
        term = jnp.dot(part_h, part_w, preferred_element_type=jnp.float32)
        rounded = lax.optimization_barrier(term.astype(jnp.bfloat16))
        return total + rounded.astype(jnp.float32)

    zeros = jnp.zeros((hidden.shape[0], down.shape[1]), jnp.float32)
    return lax.fori_loop(0, N_TP, add, zeros)


def swiglu(rows, gate_w, up_w):
    gate = jnp.dot(rows, gate_w, preferred_element_type=jnp.float32)
    up = jnp.dot(rows, up_w, preferred_element_type=jnp.float32)
    return (jax.nn.silu(gate) * up).astype(jnp.bfloat16)


def reference(tokens, routes, combine, expert_slot, dense_gate, dense_up, dense_down, expert_gate, expert_up, expert_down):
    dense_hidden = swiglu(tokens, dense_gate, dense_up)
    dense_out = group_sum(dense_hidden, dense_down)

    ids = routes.reshape(N_EP, 2 * TOK_DEV).astype(jnp.int32)
    onehot = (ids[:, :, None] == jnp.arange(EXPERTS, dtype=jnp.int32)[None, None, :]).astype(jnp.int32)
    rank = jnp.cumsum(onehot, axis=1) - 1
    pos = jnp.sum(onehot * rank, axis=2).astype(jnp.int32)
    dest = expert_slot[ids].astype(jnp.int32)
    source = jnp.arange(N_EP, dtype=jnp.int32)[:, None]
    flat = (dest * N_EP + source) * CAP + pos
    token_global = source * TOK_DEV + jnp.arange(2 * TOK_DEV, dtype=jnp.int32)[None, :] // 2
    table = jnp.full((N_EP * N_EP * CAP,), TOKENS, jnp.int32)
    table = table.at[flat.reshape(-1)].set(token_global.reshape(-1).astype(jnp.int32))
    table = table.reshape(N_EP, N_EP * CAP)
    padded = jnp.concatenate([tokens, jnp.zeros((1, D), tokens.dtype)], axis=0)

    def run_block(block):
        rows = padded[table[block]]
        hidden = swiglu(rows, expert_gate[block], expert_up[block])
        return group_sum(hidden, expert_down[block]).astype(jnp.bfloat16)

    results = lax.map(run_block, jnp.arange(N_EP, dtype=jnp.int32))
    picked = results[dest, source * CAP + pos]
    picked = picked.reshape(TOKENS, 2, D).astype(jnp.float32)
    expert_mix = jnp.sum(picked * combine[:, :, None], axis=1)
    total = tokens.astype(jnp.float32) + dense_out + expert_mix
    return total.astype(jnp.bfloat16)
```

```python
import jax
import jax.numpy as jnp
from jax import lax
from jax.experimental import pallas as pl
from jax.experimental.pallas import tpu as pltpu
from jax.sharding import PartitionSpec as P

MESH = pl.DeviceIdType.MESH
BF16 = jnp.bfloat16
F32 = jnp.float32

NR = 4
NZL = 2
CAP = 24
PAIR = 2 * CAP
ROWS = NR * NR * PAIR
CH = NR * PAIR
HALF = CH // 2
N_SEM = 160

A2A, META, TOK, INFO, AG, WZ, WY, WS, RS, RET, SIB = 0, 16, 32, 33, 34, 70, 74, 90, 106, 142, 158


def dot(a, b):
    return jnp.dot(a, b, preferred_element_type=F32)


def dot_nt(a, b):
    return lax.dot_general(a, b, (((1,), (1,)), ((), ())), preferred_element_type=F32)


def silu(v):
    return v / (1.0 + jnp.exp(-v))


def kernel(
    tokens,
    routes,
    combine,
    slots,
    dense_gate,
    dense_up,
    dense_down,
    expert_gate,
    expert_up,
    expert_down,
    out,
    tok,
    info,
    meta_out,
    meta_in,
    scale_e,
    scale_d,
    w_gate,
    w_up,
    w_down,
    w_all,
    outgoing,
    x_all,
    acc_g,
    acc_u,
    hidden,
    rs_send,
    rs_half,
    rs_full,
    rs_z,
    result,
    returned,
    part_send,
    part_recv,
    part_own,
    send_sem,
    recv_sem,
    load_sem,
):
    n_tok, width = tokens.shape
    ff = w_gate.shape[1]
    piece = dense_gate.shape[0]
    tp = lax.axis_index("tp")
    ep = lax.axis_index("ep")
    x, zl = tp % NR, tp // NR
    core, zh, y = ep % 2, (ep // 2) % NR, ep // (2 * NR)

    def at_x(d):
        return {"tp": zl * NR + (x + d + NR) % NR, "ep": ep}

    def at_chip(dy, dz):
        return {"tp": tp, "ep": ((y + dy + NR) % NR) * (2 * NR) + ((zh + dz + NR) % NR) * 2 + core}

    partner = {"tp": (1 - zl) * NR + x, "ep": ep}
    sibling = {"tp": tp, "ep": ep + 1 - 2 * core}

    sent = {}

    def send(number, src, dst, device):
        copy = pltpu.make_async_remote_copy(
            src_ref=src,
            dst_ref=dst,
            send_sem=send_sem.at[number],
            recv_sem=recv_sem.at[number],
            device_id=device,
            device_id_type=MESH,
        )
        copy.start()
        sent[number] = copy

    def arrived(number):
        sent[number].wait_recv()

    loads = []

    def load(src, dst):
        copy = pltpu.make_async_copy(src, dst, load_sem.at[len(loads)])
        copy.start()
        loads.append(copy)

    load(tokens, tok.at[core])
    load(dense_gate, w_all.at[0, 0])
    load(dense_up, w_all.at[0, 1])
    for j in range(ff // 128):
        load(dense_down.at[pl.ds(128 * j, 128), :], w_all.at[0, 2, :, pl.ds(128 * j, 128)])
    n_dense = len(loads)
    load(expert_gate.at[0], w_gate)
    load(expert_up.at[0], w_up)
    load(expert_down.at[0], w_down)

    peers = [partner, sibling, at_x(1), at_x(-1)]
    peers += [at_chip(dy, dz) for dz in range(NR) for dy in range(NR) if dy or dz]
    barrier = pltpu.get_barrier_semaphore()
    for peer in peers:
        pl.semaphore_signal(barrier, inc=1, device_id=peer, device_id_type=MESH)

    route = routes[...]
    lanes = lax.broadcasted_iota(jnp.int32, (n_tok, slots.shape[1]), 1)
    picks = [(route[:, k : k + 1] == lanes).astype(F32) for k in range(2)]
    row_id = lax.broadcasted_iota(jnp.int32, (n_tok, n_tok), 0)
    col_id = lax.broadcasted_iota(jnp.int32, (n_tok, n_tok), 1)
    before = (col_id < row_id).astype(BF16)
    eye = (col_id == row_id).astype(F32)
    earlier = dot(before, (picks[0] + picks[1]).astype(BF16))
    slot_row = slots[...].astype(F32)
    columns = []
    for k in range(2):
        pos = jnp.sum(picks[k] * earlier, axis=1, keepdims=True).astype(jnp.int32)
        dest = jnp.sum(picks[k] * slot_row, axis=1, keepdims=True).astype(jnp.int32)
        rel_z = (zh - ((dest >> 1) & (NR - 1)) + NR) & (NR - 1)
        rel_y = (y - (dest >> 3) + NR) & (NR - 1)
        place = (dest & 1) * ROWS + (rel_z * NR + rel_y) * PAIR + core * CAP + pos
        columns.append(place.astype(F32))
    for k in range(2):
        columns.append(combine[:, k : k + 1])
    for number, column in enumerate(columns):
        info[core, number : number + 1, :] = jnp.sum(eye * column, axis=0, keepdims=True)

    pl.semaphore_wait(barrier, len(peers))
    loads[0].wait()
    send(TOK, tok.at[core], tok.at[core], sibling)
    send(INFO, info.at[core], info.at[core], sibling)
    for copy in loads[1:n_dense]:
        copy.wait()

    def w_slot(dz, dy, dc):
        return (dz * NR + dy) * 2 + dc

    hp = piece // 2

    def w_send(number, slot, target, device, half=None):
        if half is None:
            send(number, w_all.at[slot], w_all.at[target], device)
        else:
            rows = pl.ds(half * hp, hp)
            send(number, w_all.at[slot, :, rows, :], w_all.at[target, :, rows, :], device)

    def w_spread(dz):
        slot = w_slot(dz, 0, 0)
        w_send(WY + 4 * dz, slot, w_slot(dz, 3, 0), at_chip(1, 0))
        w_send(WY + 4 * dz + 1, slot, w_slot(dz, 1, 0), at_chip(-1, 0))

    def w_sibling(dz, dy):
        w_send(WS + dz * NR + dy, w_slot(dz, dy, 0), w_slot(dz, dy, 1), sibling)

    def w_across(dz):
        arrived(WY + 4 * dz)
        w_send(WY + 4 * dz + 2, w_slot(dz, 3, 0), w_slot(dz, 2, 0), at_chip(1, 0), 0)
        arrived(WY + 4 * dz + 1)
        w_send(WY + 4 * dz + 3, w_slot(dz, 1, 0), w_slot(dz, 2, 0), at_chip(-1, 0), 1)
        w_sibling(dz, 3)
        w_sibling(dz, 1)

    def w_last(dz):
        arrived(WY + 4 * dz + 2)
        arrived(WY + 4 * dz + 3)
        w_sibling(dz, 2)

    def w0():
        w_spread(0)
        w_send(WZ, w_slot(0, 0, 0), w_slot(3, 0, 0), at_chip(0, 1))
        w_send(WZ + 1, w_slot(0, 0, 0), w_slot(1, 0, 0), at_chip(0, -1))
        w_sibling(0, 0)

    def w1():
        arrived(WZ)
        w_send(WZ + 2, w_slot(3, 0, 0), w_slot(2, 0, 0), at_chip(0, 1), 0)
        arrived(WZ + 1)
        w_send(WZ + 3, w_slot(1, 0, 0), w_slot(2, 0, 0), at_chip(0, -1), 1)
        w_spread(3)
        w_spread(1)
        w_sibling(3, 0)
        w_sibling(1, 0)
        w_across(0)

    def w2():
        arrived(WZ + 2)
        arrived(WZ + 3)
        w_spread(2)
        w_sibling(2, 0)
        w_last(0)
        w_across(3)
        w_across(1)

    def w3():
        w_across(2)
        w_last(3)
        w_last(1)

    def w4():
        w_last(2)

    def w5():
        for number in range(NR * NR):
            arrived(WS + number)

    arrived(TOK)
    arrived(INFO)
    place = [
        jnp.concatenate([info[b, k : k + 1, :] for b in range(2)], axis=1).astype(jnp.int32) - core * ROWS
        for k in range(2)
    ]
    weight = [jnp.concatenate([info[b, 2 + k : 3 + k, :] for b in range(2)], axis=1) for k in range(2)]
    both = jnp.concatenate([tok[0], tok[1]], axis=0)
    zero_row = jnp.zeros((1, 2 * n_tok), F32)
    tables = []
    for k in range(2):
        high = weight[k].astype(BF16).astype(F32)
        rest = weight[k] - high
        middle = rest.astype(BF16).astype(F32)
        low = rest - middle
        first = zero_row + (1.0 - k)
        tables.append(jnp.concatenate([high, middle, low, first] + [zero_row] * 4, axis=0).astype(BF16))

    for g in range(NR):
        rows = lax.broadcasted_iota(jnp.int32, (CH, 2 * n_tok), 0) + g * CH
        picks = [(place[k] == rows).astype(F32) for k in range(2)]
        block = dot((picks[0] + picks[1]).astype(BF16), both).astype(BF16)
        marks = dot_nt(tables[0], picks[0].astype(BF16)) + dot_nt(tables[1], picks[1].astype(BF16))
        for dy in range(NR):
            n = g * NR + dy
            mark = marks[:, dy * PAIR : (dy + 1) * PAIR]
            if n == 0:
                x_all[0, 0:PAIR, :] = block[0:PAIR]
                meta_in[0, :, 0:PAIR] = mark
            else:
                meta_out[n, :, 0:PAIR] = mark
        if g == 0:
            outgoing[PAIR:CH, :] = block[PAIR:CH]
        else:
            outgoing[g * CH : (g + 1) * CH, :] = block
        for dy in range(NR):
            n = g * NR + dy
            if n:
                span = pl.ds(n * PAIR, PAIR)
                send(A2A + n, outgoing.at[span, :], x_all.at[0, span, :], at_chip(-dy, -g))
                send(META + n, meta_out.at[n], meta_in.at[n], at_chip(-dy, -g))

    w0()

    def ag_send(g, number, slot, target, device, half=None):
        if half is None:
            rows = pl.ds(g * CH, CH)
        else:
            rows = pl.ds(g * CH + half * HALF, HALF)
        send(AG + 9 * g + number, x_all.at[slot, rows, :], x_all.at[target, rows, :], device)

    def ag_arrived(g, number):
        arrived(AG + 9 * g + number)

    def s1(g):
        for dy in range(NR):
            if g * NR + dy:
                arrived(A2A + g * NR + dy)
        ag_send(g, 0, 0, 4, partner)
        ag_send(g, 1, 0, 3, at_x(1))
        ag_send(g, 2, 0, 1, at_x(-1))

    def s2(g):
        ag_arrived(g, 0)
        ag_send(g, 3, 4, 7, at_x(1))
        ag_send(g, 4, 4, 5, at_x(-1))
        ag_arrived(g, 1)
        ag_send(g, 5, 3, 2, at_x(1), 0)
        ag_arrived(g, 2)
        ag_send(g, 6, 1, 2, at_x(-1), 1)

    def s3(g):
        ag_arrived(g, 3)
        ag_send(g, 7, 7, 6, at_x(1), 0)
        ag_arrived(g, 4)
        ag_send(g, 8, 5, 6, at_x(-1), 1)

    def tp_of(slot):
        return ((zl + slot // NR) % NZL) * NR + (x + slot % NR) % NR

    def dense_slots(t):
        found = []
        for j in range(4):
            e = t * 4 + j
            dz = ((e // 2) % NR - zh + NR) % NR
            dy = (e // (2 * NR) - y + NR) % NR
            dc = (j % 2 + core) % 2
            found.append(w_slot(dz, dy, dc))
        return found

    def s4(g):
        for number in range(5, 9):
            ag_arrived(g, number)
        acc_g[g] = jnp.zeros((CH, ff), F32)
        acc_u[g] = jnp.zeros((CH, ff), F32)

        def step(slot, _):
            part = x_all[slot, pl.ds(g * CH, CH), :]
            rows = pl.ds(pl.multiple_of(tp_of(slot) * width, width), width)
            acc_g[g] += dot(part, w_gate[rows, :])
            acc_u[g] += dot(part, w_up[rows, :])
            return 0

        lax.fori_loop(0, NZL * NR, step, 0)
        spread = jnp.concatenate([scale_e[g * CH : (g + 1) * CH, :]] * (ff // 128), axis=1)
        hidden[g, :, 0:ff] = (silu(acc_g[g]) * acc_u[g] * spread).astype(BF16)

    def dense(g):
        acc_g[g] = jnp.zeros((CH, ff), F32)
        acc_u[g] = jnp.zeros((CH, ff), F32)

        def step(slot, _):
            part = x_all[slot, pl.ds(g * CH, CH), :]
            found = dense_slots(tp_of(slot))
            acc_g[g] += dot(part, jnp.concatenate([w_all[s, 0] for s in found], axis=0))
            acc_u[g] += dot(part, jnp.concatenate([w_all[s, 1] for s in found], axis=0))
            return 0

        lax.fori_loop(0, NZL * NR, step, 0)
        spread = jnp.concatenate([scale_d[g * CH : (g + 1) * CH, :]] * (ff // 128), axis=1)
        hidden[g, :, ff : 2 * ff] = (silu(acc_g[g]) * acc_u[g] * spread).astype(BF16)

    def scales():
        pick = lax.broadcasted_iota(jnp.int32, (PAIR, 128), 0) == lax.broadcasted_iota(jnp.int32, (PAIR, 128), 1)
        for n in range(NR * NR):
            if n:
                arrived(META + n)
            mark = meta_in[n]
            value = mark[0:1] + mark[1:2] + mark[2:3]
            first = mark[3:4]
            for row, target in ((value, scale_e), (first, scale_d)):
                column = jnp.sum(jnp.where(pick, row, 0.0), axis=1, keepdims=True)
                target[n * PAIR : (n + 1) * PAIR, :] = jnp.broadcast_to(column, (PAIR, 128))

    s1(0)
    s1(1)
    s2(0)
    w1()
    s1(3)
    s2(1)
    s3(0)
    scales()
    for copy in loads[n_dense:]:
        copy.wait()
    w2()
    s1(2)
    s2(3)
    s3(1)
    s4(0)
    w3()
    s2(2)
    s3(3)
    s4(1)
    w4()
    s3(2)
    s4(3)
    s4(2)
    w5()

    def down(g, dz, dx):
        t = ((zl + dz) % NZL) * NR + (x + dx) % NR
        cols = pl.ds(pl.multiple_of(t * width, width), width)
        blocks = []
        for s in dense_slots(t):
            block = w_all[s, 2]
            blocks.append(jnp.concatenate([block[:, 128 * j : 128 * (j + 1)] for j in range(ff // 128)], axis=0))
        weights = jnp.concatenate([w_down[:, cols], jnp.concatenate(blocks, axis=1)], axis=0)
        return dot(hidden[g], weights)

    def rs_number(g, number):
        return RS + 9 * g + number

    def r1(g):
        for dz in (1, 0):
            rs_send[g, 3 * dz] = down(g, dz, 2).astype(BF16)
            send(rs_number(g, 4 * dz), rs_send.at[g, 3 * dz, pl.ds(0, HALF), :], rs_half.at[g, 2 * dz], at_x(1))
            send(
                rs_number(g, 4 * dz + 1),
                rs_send.at[g, 3 * dz, pl.ds(HALF, HALF), :],
                rs_half.at[g, 2 * dz + 1],
                at_x(-1),
            )

    def r2(g):
        for dz in (1, 0):
            part = down(g, dz, 1)
            arrived(rs_number(g, 4 * dz))
            rs_send[g, 3 * dz + 1, 0:HALF, :] = (part[0:HALF] + rs_half[g, 2 * dz].astype(F32)).astype(BF16)
            rs_send[g, 3 * dz + 1, HALF:CH, :] = part[HALF:CH].astype(BF16)
            send(rs_number(g, 4 * dz + 2), rs_send.at[g, 3 * dz + 1], rs_full.at[g, 2 * dz], at_x(1))
            part = down(g, dz, 3)
            arrived(rs_number(g, 4 * dz + 1))
            rs_send[g, 3 * dz + 2, 0:HALF, :] = part[0:HALF].astype(BF16)
            rs_send[g, 3 * dz + 2, HALF:CH, :] = (part[HALF:CH] + rs_half[g, 2 * dz + 1].astype(F32)).astype(BF16)
            send(rs_number(g, 4 * dz + 3), rs_send.at[g, 3 * dz + 2], rs_full.at[g, 2 * dz + 1], at_x(-1))

    def gathered(g, dz):
        part = down(g, dz, 0)
        arrived(rs_number(g, 4 * dz + 2))
        arrived(rs_number(g, 4 * dz + 3))
        return part + rs_full[g, 2 * dz].astype(F32) + rs_full[g, 2 * dz + 1].astype(F32)

    def r3(g):
        rs_send[g, 6] = gathered(g, 1).astype(BF16)
        send(rs_number(g, 8), rs_send.at[g, 6], rs_z.at[g], partner)

    def r4(g):
        total = gathered(g, 0)
        arrived(rs_number(g, 8))
        total = (total + rs_z[g].astype(F32)).astype(BF16)
        if g == 0:
            returned[0:PAIR, :] = total[0:PAIR]
            result[PAIR:CH, :] = total[PAIR:CH]
        else:
            result[g * CH : (g + 1) * CH, :] = total
        for dy in range(NR):
            n = g * NR + dy
            if n:
                span = pl.ds(n * PAIR, PAIR)
                send(RET + n, result.at[span, :], returned.at[span, :], at_chip(dy, g))

    a, b, c, d = 1, 3, 2, 0
    dense(a)
    r1(a)
    dense(b)
    r1(b)
    r2(a)
    dense(c)
    r1(c)
    r2(b)
    r3(a)
    dense(d)
    r1(d)
    r2(c)
    r3(b)
    r4(a)
    r2(d)
    r3(c)
    r4(b)
    r3(d)
    r4(c)
    r4(d)

    def column(b, k):
        row = info[b, k : k + 1, :]
        return jnp.sum(eye * row, axis=1, keepdims=True).astype(jnp.int32) - core * ROWS

    other = 1 - core
    own_cols = [column(core, k) for k in range(2)]
    other_cols = [column(other, k) for k in range(2)]
    part_send[...] = jnp.zeros_like(part_send)
    part_own[...] = tok[core].astype(F32)
    for g in (a, b, c, d):
        for dy in range(NR):
            if g * NR + dy:
                arrived(RET + g * NR + dy)
        rows = lax.broadcasted_iota(jnp.int32, (n_tok, CH), 1) + g * CH
        block = returned[g * CH : (g + 1) * CH, :]
        for cols, target in ((other_cols, part_send), (own_cols, part_own)):
            chosen = (cols[0] == rows).astype(F32) + (cols[1] == rows).astype(F32)
            target[...] += dot(chosen.astype(BF16), block)
    send(SIB, part_send, part_recv, sibling)
    arrived(SIB)
    out[...] = (part_own[...] + part_recv[...]).astype(BF16)

    for copy in sent.values():
        copy.wait_send()


def body(tokens, routes, combine, expert_slot, dense_gate, dense_up, dense_down, expert_gate, expert_up, expert_down):
    n_tok, width = tokens.shape
    depth, ff = expert_gate.shape[1:]
    piece = dense_gate.shape[0]
    any_spec = pl.BlockSpec(memory_space=pl.ANY)
    vmem = pl.BlockSpec(memory_space=pltpu.VMEM)
    n_slots = NZL * NR
    return pl.pallas_call(
        kernel,
        out_shape=jax.ShapeDtypeStruct((n_tok, width), BF16),
        in_specs=[any_spec, vmem, vmem, vmem] + [any_spec] * 6,
        out_specs=vmem,
        scratch_shapes=[
            pltpu.VMEM((2, n_tok, width), BF16),
            pltpu.VMEM((2, 8, n_tok), F32),
            pltpu.VMEM((NR * NR, 8, 128), F32),
            pltpu.VMEM((NR * NR, 8, 128), F32),
            pltpu.VMEM((ROWS, 128), F32),
            pltpu.VMEM((ROWS, 128), F32),
            pltpu.VMEM((depth, ff), BF16),
            pltpu.VMEM((depth, ff), BF16),
            pltpu.VMEM((ff, depth), BF16),
            pltpu.VMEM((2 * NR * NR, 3, piece, ff), BF16),
            pltpu.VMEM((ROWS, width), BF16),
            pltpu.VMEM((n_slots, ROWS, width), BF16),
            pltpu.VMEM((NR, CH, ff), F32),
            pltpu.VMEM((NR, CH, ff), F32),
            pltpu.VMEM((NR, CH, 2 * ff), BF16),
            pltpu.VMEM((NR, 7, CH, width), BF16),
            pltpu.VMEM((NR, 4, HALF, width), BF16),
            pltpu.VMEM((NR, 4, CH, width), BF16),
            pltpu.VMEM((NR, CH, width), BF16),
            pltpu.VMEM((ROWS, width), BF16),
            pltpu.VMEM((ROWS, width), BF16),
            pltpu.VMEM((n_tok, width), F32),
            pltpu.VMEM((n_tok, width), F32),
            pltpu.VMEM((n_tok, width), F32),
            pltpu.SemaphoreType.DMA((N_SEM,)),
            pltpu.SemaphoreType.DMA((N_SEM,)),
            pltpu.SemaphoreType.DMA((9,)),
        ],
        compiler_params=pltpu.CompilerParams(
            collective_id=0, has_side_effects=True, vmem_limit_bytes=60 * 1024 * 1024
        ),
    )(
        tokens,
        routes,
        combine,
        expert_slot.reshape(1, -1),
        dense_gate,
        dense_up,
        dense_down,
        expert_gate,
        expert_up,
        expert_down,
    )


def solution(mesh):
    in_specs = (
        P("ep", "tp"),
        P("ep", None),
        P("ep", None),
        P(),
        P("ep", "tp"),
        P("ep", "tp"),
        P("tp", "ep"),
        P("ep", None, "tp"),
        P("ep", None, "tp"),
        P("ep", "tp", None),
    )
    out_specs = P("ep", "tp")
    return jax.shard_map(body, mesh=mesh, in_specs=in_specs, out_specs=out_specs, check_vma=False)
```

```python
import jax
import jax.numpy as jnp
from jax import lax
from jax.experimental import pallas as pl
from jax.experimental.pallas import tpu as pltpu
from jax.sharding import PartitionSpec as P

MESH = pl.DeviceIdType.MESH
BF16 = jnp.bfloat16
F32 = jnp.float32

NR = 4
NZL = 2
CAP = 24
PAIR = 2 * CAP
ROWS = NR * NR * PAIR
CH = NR * PAIR
HALF = CH // 2
N_SEM = 160

A2A, META, TOK, INFO, AG, WZ, WY, WS, RS, RET, SIB = 0, 16, 32, 33, 34, 70, 74, 90, 106, 142, 158


def dot(a, b):
    return jnp.dot(a, b, preferred_element_type=F32)


def dot_nt(a, b):
    return lax.dot_general(a, b, (((1,), (1,)), ((), ())), preferred_element_type=F32)


def silu(v):
    return v / (1.0 + jnp.exp(-v))


def kernel(
    tokens,
    routes,
    combine,
    slots,
    dense_gate,
    dense_up,
    dense_down,
    expert_gate,
    expert_up,
    expert_down,
    out,
    tok,
    info,
    meta_out,
    meta_in,
    scale_e,
    scale_d,
    w_gate,
    w_up,
    w_down,
    w_all,
    outgoing,
    x_all,
    acc_g,
    acc_u,
    hidden,
    rs_send,
    rs_half,
    rs_full,
    rs_z,
    result,
    returned,
    part_send,
    part_recv,
    part_own,
    send_sem,
    recv_sem,
    load_sem,
):
    n_tok, width = tokens.shape
    n_slot = slots.shape[1]
    ff = w_gate.shape[1]
    piece = dense_gate.shape[0]
    tp = lax.axis_index("tp")
    ep = lax.axis_index("ep")
    x, zl = tp % NR, tp // NR
    core, zh, y = ep % 2, (ep // 2) % NR, ep // (2 * NR)

    def at_x(d):
        return {"tp": zl * NR + (x + d + NR) % NR, "ep": ep}

    def at_chip(dy, dz):
        return {"tp": tp, "ep": ((y + dy + NR) % NR) * (2 * NR) + ((zh + dz + NR) % NR) * 2 + core}

    partner = {"tp": (1 - zl) * NR + x, "ep": ep}
    sibling = {"tp": tp, "ep": ep + 1 - 2 * core}

    sent = {}

    def send(number, src, dst, device):
        copy = pltpu.make_async_remote_copy(
            src_ref=src,
            dst_ref=dst,
            send_sem=send_sem.at[number],
            recv_sem=recv_sem.at[number],
            device_id=device,
            device_id_type=MESH,
        )
        copy.start()
        sent[number] = copy

    def arrived(number):
        sent[number].wait_recv()

    loads = []

    def load(src, dst):
        copy = pltpu.make_async_copy(src, dst, load_sem.at[len(loads)])
        copy.start()
        loads.append(copy)

    load(tokens, tok.at[core])
    load(dense_gate, w_all.at[0, 0])
    load(dense_up, w_all.at[0, 1])
    for j in range(ff // 128):
        load(dense_down.at[pl.ds(128 * j, 128), :], w_all.at[0, 2, :, pl.ds(128 * j, 128)])
    n_dense = len(loads)
    load(expert_gate.at[0], w_gate)
    load(expert_up.at[0], w_up)
    load(expert_down.at[0], w_down)

    peers = [partner, sibling, at_x(1), at_x(-1)]
    peers += [at_chip(dy, dz) for dz in range(NR) for dy in range(NR) if dy or dz]
    barrier = pltpu.get_barrier_semaphore()
    for peer in peers:
        pl.semaphore_signal(barrier, inc=1, device_id=peer, device_id_type=MESH)

    experts = lax.broadcasted_iota(jnp.int32, (n_slot, n_tok), 0)
    picks = [(routes[k : k + 1, :] == experts).astype(F32) for k in range(2)]
    row_id = lax.broadcasted_iota(jnp.int32, (n_tok, n_tok), 0)
    col_id = lax.broadcasted_iota(jnp.int32, (n_tok, n_tok), 1)
    before = (row_id < col_id).astype(BF16)
    earlier = dot((picks[0] + picks[1]).astype(BF16), before)
    same = lax.broadcasted_iota(jnp.int32, (n_slot, n_slot), 0) == lax.broadcasted_iota(jnp.int32, (n_slot, n_slot), 1)
    slot_of = jnp.sum(jnp.where(same, slots[...].astype(F32), 0.0), axis=1, keepdims=True)
    for k in range(2):
        pos = jnp.sum(picks[k] * earlier, axis=0, keepdims=True).astype(jnp.int32)
        dest = jnp.sum(picks[k] * slot_of, axis=0, keepdims=True).astype(jnp.int32)
        rel_z = (zh - ((dest >> 1) & (NR - 1)) + NR) & (NR - 1)
        rel_y = (y - (dest >> 3) + NR) & (NR - 1)
        place = (dest & 1) * ROWS + (rel_z * NR + rel_y) * PAIR + core * CAP + pos
        info[core, k : k + 1, :] = place.astype(F32)
        info[core, 2 + k : 3 + k, :] = combine[k : k + 1, :]

    pl.semaphore_wait(barrier, len(peers))
    loads[0].wait()
    send(TOK, tok.at[core], tok.at[core], sibling)
    send(INFO, info.at[core], info.at[core], sibling)
    for copy in loads[1:n_dense]:
        copy.wait()

    def w_slot(dz, dy, dc):
        return (dz * NR + dy) * 2 + dc

    hp = piece // 2

    def w_send(number, slot, target, device, half=None):
        if half is None:
            send(number, w_all.at[slot], w_all.at[target], device)
        else:
            rows = pl.ds(half * hp, hp)
            send(number, w_all.at[slot, :, rows, :], w_all.at[target, :, rows, :], device)

    def w_spread(dz):
        slot = w_slot(dz, 0, 0)
        w_send(WY + 4 * dz, slot, w_slot(dz, 3, 0), at_chip(1, 0))
        w_send(WY + 4 * dz + 1, slot, w_slot(dz, 1, 0), at_chip(-1, 0))

    def w_sibling(dz, dy):
        w_send(WS + dz * NR + dy, w_slot(dz, dy, 0), w_slot(dz, dy, 1), sibling)

    def w_across(dz, back):
        dy = 1 if back else 3
        arrived(WY + 4 * dz + back)
        w_send(WY + 4 * dz + 2 + back, w_slot(dz, dy, 0), w_slot(dz, 2, 0), at_chip(1 - 2 * back, 0), back)
        w_sibling(dz, dy)

    def w_last(dz):
        arrived(WY + 4 * dz + 2)
        arrived(WY + 4 * dz + 3)
        w_sibling(dz, 2)

    def w_start():
        w_send(WZ, w_slot(0, 0, 0), w_slot(3, 0, 0), at_chip(0, 1))
        w_send(WZ + 1, w_slot(0, 0, 0), w_slot(1, 0, 0), at_chip(0, -1))
        w_sibling(0, 0)

    def w_next(dz):
        arrived(WZ + (0 if dz == 3 else 1))
        w_spread(dz)
        w_sibling(dz, 0)

    def w_half(back):
        w_send(WZ + 2 + back, w_slot(1 if back else 3, 0, 0), w_slot(2, 0, 0), at_chip(0, 1 - 2 * back), back)

    def w_far():
        arrived(WZ + 2)
        arrived(WZ + 3)
        w_spread(2)
        w_sibling(2, 0)

    def w5():
        for number in range(NR * NR):
            arrived(WS + number)

    arrived(TOK)
    arrived(INFO)
    place = [
        jnp.concatenate([info[b, k : k + 1, :] for b in range(2)], axis=1).astype(jnp.int32) - core * ROWS
        for k in range(2)
    ]
    weight = [jnp.concatenate([info[b, 2 + k : 3 + k, :] for b in range(2)], axis=1) for k in range(2)]
    both = jnp.concatenate([tok[0], tok[1]], axis=0)
    zero_row = jnp.zeros((1, 2 * n_tok), F32)
    tables = []
    for k in range(2):
        high = weight[k].astype(BF16).astype(F32)
        rest = weight[k] - high
        middle = rest.astype(BF16).astype(F32)
        low = rest - middle
        first = zero_row + (1.0 - k)
        tables.append(jnp.concatenate([high, middle, low, first] + [zero_row] * 4, axis=0).astype(BF16))

    def pack(g):
        rows = lax.broadcasted_iota(jnp.int32, (CH, 2 * n_tok), 0) + g * CH
        picks = [(place[k] == rows).astype(F32) for k in range(2)]
        block = dot((picks[0] + picks[1]).astype(BF16), both).astype(BF16)
        marks = dot_nt(tables[0], picks[0].astype(BF16)) + dot_nt(tables[1], picks[1].astype(BF16))
        for dy in range(NR):
            n = g * NR + dy
            mark = marks[:, dy * PAIR : (dy + 1) * PAIR]
            if n == 0:
                x_all[0, 0:PAIR, :] = block[0:PAIR]
                meta_in[0, :, 0:PAIR] = mark
            else:
                meta_out[n, :, 0:PAIR] = mark
        if g == 0:
            outgoing[PAIR:CH, :] = block[PAIR:CH]
        else:
            outgoing[g * CH : (g + 1) * CH, :] = block

    def dispatch(g):
        for dy in range(NR):
            n = g * NR + dy
            if n:
                span = pl.ds(n * PAIR, PAIR)
                send(A2A + n, outgoing.at[span, :], x_all.at[0, span, :], at_chip(-dy, -g))
                send(META + n, meta_out.at[n], meta_in.at[n], at_chip(-dy, -g))

    def ag_send(g, number, slot, target, device, half=None):
        if half is None:
            rows = pl.ds(g * CH, CH)
        else:
            rows = pl.ds(g * CH + half * HALF, HALF)
        send(AG + 9 * g + number, x_all.at[slot, rows, :], x_all.at[target, rows, :], device)

    def ag_arrived(g, number):
        arrived(AG + 9 * g + number)

    def s1(g):
        for dy in range(NR):
            if g * NR + dy:
                arrived(A2A + g * NR + dy)
        ag_send(g, 0, 0, 4, partner)
        ag_send(g, 1, 0, 3, at_x(1))
        ag_send(g, 2, 0, 1, at_x(-1))

    def s2b(g):
        ag_arrived(g, 0)
        ag_send(g, 3, 4, 7, at_x(1))
        ag_send(g, 4, 4, 5, at_x(-1))

    def s2a(g, back):
        ag_arrived(g, 1 + back)
        ag_send(g, 5 + back, 1 if back else 3, 2, at_x(1 - 2 * back), back)

    def s3(g, back):
        ag_arrived(g, 3 + back)
        ag_send(g, 7 + back, 5 if back else 7, 6, at_x(1 - 2 * back), back)

    def tp_of(slot):
        return ((zl + slot // NR) % NZL) * NR + (x + slot % NR) % NR

    def dense_slots(t):
        found = []
        for j in range(4):
            e = t * 4 + j
            dz = ((e // 2) % NR - zh + NR) % NR
            dy = (e // (2 * NR) - y + NR) % NR
            dc = (j % 2 + core) % 2
            found.append(w_slot(dz, dy, dc))
        return found

    def s4(g):
        for number in range(5, 9):
            ag_arrived(g, number)
        acc_g[g] = jnp.zeros((CH, ff), F32)
        acc_u[g] = jnp.zeros((CH, ff), F32)

        def step(slot, _):
            part = x_all[slot, pl.ds(g * CH, CH), :]
            rows = pl.ds(pl.multiple_of(tp_of(slot) * width, width), width)
            acc_g[g] += dot(part, w_gate[rows, :])
            acc_u[g] += dot(part, w_up[rows, :])
            return 0

        lax.fori_loop(0, NZL * NR, step, 0)
        spread = jnp.concatenate([scale_e[g * CH : (g + 1) * CH, :]] * (ff // 128), axis=1)
        hidden[g, :, 0:ff] = (silu(acc_g[g]) * acc_u[g] * spread).astype(BF16)

    def dense(g):
        acc_g[g] = jnp.zeros((CH, ff), F32)
        acc_u[g] = jnp.zeros((CH, ff), F32)

        def step(slot, _):
            part = x_all[slot, pl.ds(g * CH, CH), :]
            found = dense_slots(tp_of(slot))
            acc_g[g] += dot(part, jnp.concatenate([w_all[s, 0] for s in found], axis=0))
            acc_u[g] += dot(part, jnp.concatenate([w_all[s, 1] for s in found], axis=0))
            return 0

        lax.fori_loop(0, NZL * NR, step, 0)
        spread = jnp.concatenate([scale_d[g * CH : (g + 1) * CH, :]] * (ff // 128), axis=1)
        hidden[g, :, ff : 2 * ff] = (silu(acc_g[g]) * acc_u[g] * spread).astype(BF16)

    def scales():
        pick = lax.broadcasted_iota(jnp.int32, (PAIR, 128), 0) == lax.broadcasted_iota(jnp.int32, (PAIR, 128), 1)
        for n in range(NR * NR):
            if n:
                arrived(META + n)
            mark = meta_in[n]
            value = mark[0:1] + mark[1:2] + mark[2:3]
            first = mark[3:4]
            for row, target in ((value, scale_e), (first, scale_d)):
                column = jnp.sum(jnp.where(pick, row, 0.0), axis=1, keepdims=True)
                target[n * PAIR : (n + 1) * PAIR, :] = jnp.broadcast_to(column, (PAIR, 128))

    def down(g, dz, dx):
        t = ((zl + dz) % NZL) * NR + (x + dx) % NR
        cols = pl.ds(pl.multiple_of(t * width, width), width)
        blocks = []
        for s in dense_slots(t):
            block = w_all[s, 2]
            blocks.append(jnp.concatenate([block[:, 128 * j : 128 * (j + 1)] for j in range(ff // 128)], axis=0))
        weights = jnp.concatenate([w_down[:, cols], jnp.concatenate(blocks, axis=1)], axis=0)
        return dot(hidden[g], weights)

    def rs_number(g, number):
        return RS + 9 * g + number

    def r1(g, dz):
        rs_send[g, 3 * dz] = down(g, dz, 2).astype(BF16)
        for back in range(2):
            rows = pl.ds(back * HALF, HALF)
            target = rs_half.at[g, 2 * dz + back]
            send(rs_number(g, 4 * dz + back), rs_send.at[g, 3 * dz, rows, :], target, at_x(1 - 2 * back))

    def r2(g, dz, back):
        part = down(g, dz, 3 if back else 1)
        arrived(rs_number(g, 4 * dz + back))
        slot = 3 * dz + 1 + back
        near, far = back * HALF, (1 - back) * HALF
        both_rows = part[near : near + HALF] + rs_half[g, 2 * dz + back].astype(F32)
        rs_send[g, slot, near : near + HALF, :] = both_rows.astype(BF16)
        rs_send[g, slot, far : far + HALF, :] = part[far : far + HALF].astype(BF16)
        target = rs_full.at[g, 2 * dz + back]
        send(rs_number(g, 4 * dz + 2 + back), rs_send.at[g, slot], target, at_x(1 - 2 * back))

    def gathered(g, dz):
        part = down(g, dz, 0)
        arrived(rs_number(g, 4 * dz + 2))
        arrived(rs_number(g, 4 * dz + 3))
        return part + rs_full[g, 2 * dz].astype(F32) + rs_full[g, 2 * dz + 1].astype(F32)

    def r3(g):
        rs_send[g, 6] = gathered(g, 1).astype(BF16)
        send(rs_number(g, 8), rs_send.at[g, 6], rs_z.at[g], partner)

    def r4(g):
        total = gathered(g, 0)
        arrived(rs_number(g, 8))
        total = (total + rs_z[g].astype(F32)).astype(BF16)
        if g == 0:
            returned[0:PAIR, :] = total[0:PAIR]
            result[PAIR:CH, :] = total[PAIR:CH]
        else:
            result[g * CH : (g + 1) * CH, :] = total
        for dy in range(NR):
            n = g * NR + dy
            if n:
                span = pl.ds(n * PAIR, PAIR)
                send(RET + n, result.at[span, :], returned.at[span, :], at_chip(dy, g))

    eye = (col_id == row_id).astype(F32)

    def column(b, k):
        row = info[b, k : k + 1, :]
        return jnp.sum(eye * row, axis=1, keepdims=True).astype(jnp.int32) - core * ROWS

    own_cols = [column(core, k) for k in range(2)]
    other_cols = [column(1 - core, k) for k in range(2)]
    part_send[...] = jnp.zeros_like(part_send)
    part_own[...] = tok[core].astype(F32)

    def combine_rows(g):
        for dy in range(NR):
            if g * NR + dy:
                arrived(RET + g * NR + dy)
        rows = lax.broadcasted_iota(jnp.int32, (n_tok, CH), 1) + g * CH
        block = returned[g * CH : (g + 1) * CH, :]
        for cols, target in ((other_cols, part_send), (own_cols, part_own)):
            chosen = (cols[0] == rows).astype(F32) + (cols[1] == rows).astype(F32)
            target[...] += dot(chosen.astype(BF16), block)

    def exchange():
        send(SIB, part_send, part_recv, sibling)
        arrived(SIB)
        out[...] = (part_own[...] + part_recv[...]).astype(BF16)

    w_start()
    pack(3)
    pack(0)
    pack(1)
    dispatch(0)
    w_spread(0)
    dispatch(1)
    s1(0)
    dispatch(3)
    s2a(0, 0)
    s2a(0, 1)
    s1(3)
    w_next(3)
    w_across(0, 0)
    w_next(1)
    pack(2)
    s1(1)
    s2b(0)
    s2b(3)
    dispatch(2)
    w_across(3, 1)
    s2b(1)
    w_across(0, 1)
    s3(3, 0)
    s3(3, 1)
    s2a(1, 1)
    w_across(1, 1)
    s3(0, 0)
    w_half(1)
    w_half(0)
    w_across(3, 0)
    s2a(3, 0)
    s2a(3, 1)
    w_across(1, 0)
    scales()
    w_far()
    s1(2)
    for copy in loads[n_dense:]:
        copy.wait()
    s4(3)
    s3(1, 0)
    s3(0, 1)
    s2a(2, 0)
    s2b(2)
    w_across(2, 0)
    w_across(2, 1)
    w_last(3)
    w_last(1)
    s4(0)
    w_last(0)
    s3(1, 1)
    w_last(2)
    s2a(2, 1)
    s2a(1, 0)
    s3(2, 1)
    w5()
    s3(2, 0)
    dense(3)
    r1(3, 1)
    r1(3, 0)
    s4(1)
    dense(1)
    r1(1, 0)
    r2(3, 1, 0)
    r1(1, 1)
    r2(3, 1, 1)
    s4(2)
    dense(0)
    r2(1, 1, 1)
    r2(1, 1, 0)
    r3(3)
    r2(1, 0, 0)
    r2(1, 0, 1)
    dense(2)
    r3(1)
    r2(3, 0, 0)
    r1(2, 1)
    r2(3, 0, 1)
    r4(1)
    r1(0, 1)
    r2(2, 1, 1)
    r2(2, 1, 0)
    r4(3)
    r1(2, 0)
    r2(0, 1, 1)
    r2(0, 1, 0)
    r3(2)
    r2(2, 0, 0)
    r1(0, 0)
    r2(2, 0, 1)
    combine_rows(1)
    r3(0)
    r2(0, 0, 0)
    r4(2)
    r2(0, 0, 1)
    combine_rows(3)
    r4(0)
    combine_rows(0)
    combine_rows(2)
    exchange()

    for copy in sent.values():
        copy.wait_send()


def body(tokens, routes, combine, expert_slot, dense_gate, dense_up, dense_down, expert_gate, expert_up, expert_down):
    n_tok, width = tokens.shape
    depth, ff = expert_gate.shape[1:]
    piece = dense_gate.shape[0]
    any_spec = pl.BlockSpec(memory_space=pl.ANY)
    vmem = pl.BlockSpec(memory_space=pltpu.VMEM)
    n_slots = NZL * NR
    return pl.pallas_call(
        kernel,
        out_shape=jax.ShapeDtypeStruct((n_tok, width), BF16),
        in_specs=[any_spec, vmem, vmem, vmem] + [any_spec] * 6,
        out_specs=vmem,
        scratch_shapes=[
            pltpu.VMEM((2, n_tok, width), BF16),
            pltpu.VMEM((2, 8, n_tok), F32),
            pltpu.VMEM((NR * NR, 8, 128), F32),
            pltpu.VMEM((NR * NR, 8, 128), F32),
            pltpu.VMEM((ROWS, 128), F32),
            pltpu.VMEM((ROWS, 128), F32),
            pltpu.VMEM((depth, ff), BF16),
            pltpu.VMEM((depth, ff), BF16),
            pltpu.VMEM((ff, depth), BF16),
            pltpu.VMEM((2 * NR * NR, 3, piece, ff), BF16),
            pltpu.VMEM((ROWS, width), BF16),
            pltpu.VMEM((n_slots, ROWS, width), BF16),
            pltpu.VMEM((NR, CH, ff), F32),
            pltpu.VMEM((NR, CH, ff), F32),
            pltpu.VMEM((NR, CH, 2 * ff), BF16),
            pltpu.VMEM((NR, 7, CH, width), BF16),
            pltpu.VMEM((NR, 4, HALF, width), BF16),
            pltpu.VMEM((NR, 4, CH, width), BF16),
            pltpu.VMEM((NR, CH, width), BF16),
            pltpu.VMEM((ROWS, width), BF16),
            pltpu.VMEM((ROWS, width), BF16),
            pltpu.VMEM((n_tok, width), F32),
            pltpu.VMEM((n_tok, width), F32),
            pltpu.VMEM((n_tok, width), F32),
            pltpu.SemaphoreType.DMA((N_SEM,)),
            pltpu.SemaphoreType.DMA((N_SEM,)),
            pltpu.SemaphoreType.DMA((9,)),
        ],
        compiler_params=pltpu.CompilerParams(
            collective_id=0, has_side_effects=True, vmem_limit_bytes=60 * 1024 * 1024
        ),
    )(
        tokens,
        routes.T,
        combine.T,
        expert_slot.reshape(1, -1),
        dense_gate,
        dense_up,
        dense_down,
        expert_gate,
        expert_up,
        expert_down,
    )


def solution(mesh):
    in_specs = (
        P("ep", "tp"),
        P("ep", None),
        P("ep", None),
        P(),
        P("ep", "tp"),
        P("ep", "tp"),
        P("tp", "ep"),
        P("ep", None, "tp"),
        P("ep", None, "tp"),
        P("ep", "tp", None),
    )
    out_specs = P("ep", "tp")
    return jax.shard_map(body, mesh=mesh, in_specs=in_specs, out_specs=out_specs, check_vma=False)
```

```python
import jax
import jax.numpy as jnp
from jax import lax
from jax.experimental import pallas as pl
from jax.experimental.pallas import tpu as pltpu
from jax.sharding import PartitionSpec as P

MESH = pl.DeviceIdType.MESH
BF16 = jnp.bfloat16
F32 = jnp.float32

NR = 4
NZL = 2
CAP = 24
PAIR = 2 * CAP
ROWS = NR * NR * PAIR
CH = NR * PAIR
HALF = CH // 2
BY_Z = (1, 2, 3)
N_SEM = 164

A2A, META, TOK, INFO, AG, WZ, WY, WS, RS, RET, SIB, FAR = 0, 16, 32, 33, 34, 70, 74, 90, 106, 142, 158, 160


def dot(a, b):
    return jnp.dot(a, b, preferred_element_type=F32)


def dot_nt(a, b):
    return lax.dot_general(a, b, (((1,), (1,)), ((), ())), preferred_element_type=F32)


def silu(v):
    return v / (1.0 + jnp.exp(-v))


def kernel(
    tokens,
    routes,
    combine,
    slots,
    dense_gate,
    dense_up,
    dense_down,
    expert_gate,
    expert_up,
    expert_down,
    out,
    tok,
    info,
    meta_out,
    meta_in,
    scale_e,
    scale_d,
    w_gate,
    w_up,
    w_down,
    w_all,
    outgoing,
    x_all,
    hidden,
    rs_send,
    rs_half,
    rs_full,
    rs_z,
    rs_far,
    result,
    returned,
    part_send,
    part_recv,
    part_own,
    send_sem,
    recv_sem,
    load_sem,
):
    n_tok, width = tokens.shape
    n_slot = slots.shape[1]
    ff = w_gate.shape[1]
    piece = dense_gate.shape[0]
    tp = lax.axis_index("tp")
    ep = lax.axis_index("ep")
    x, zl = tp % NR, tp // NR
    core, zh, y = ep % 2, (ep // 2) % NR, ep // (2 * NR)

    def at_x(d):
        return {"tp": zl * NR + (x + d + NR) % NR, "ep": ep}

    def at_chip(dy, dz):
        return {"tp": tp, "ep": ((y + dy + NR) % NR) * (2 * NR) + ((zh + dz + NR) % NR) * 2 + core}

    partner = {"tp": (1 - zl) * NR + x, "ep": ep}
    sibling = {"tp": tp, "ep": ep + 1 - 2 * core}

    sent = {}

    def send(number, src, dst, device):
        copy = pltpu.make_async_remote_copy(
            src_ref=src,
            dst_ref=dst,
            send_sem=send_sem.at[number],
            recv_sem=recv_sem.at[number],
            device_id=device,
            device_id_type=MESH,
        )
        copy.start()
        sent[number] = copy

    def arrived(number):
        sent[number].wait_recv()

    loads = []

    def load(src, dst):
        copy = pltpu.make_async_copy(src, dst, load_sem.at[len(loads)])
        copy.start()
        loads.append(copy)

    load(tokens, tok.at[core])
    load(dense_gate, w_all.at[0, 0])
    load(dense_up, w_all.at[0, 1])
    for j in range(ff // 128):
        load(dense_down.at[pl.ds(128 * j, 128), :], w_all.at[0, 2, :, pl.ds(128 * j, 128)])
    n_dense = len(loads)
    load(expert_gate.at[0], w_gate)
    load(expert_up.at[0], w_up)
    load(expert_down.at[0], w_down)

    peers = [partner, sibling, at_x(1), at_x(-1)]
    peers += [at_chip(dy, dz) for dz in range(NR) for dy in range(NR) if dy or dz]
    barrier = pltpu.get_barrier_semaphore()
    for peer in peers:
        pl.semaphore_signal(barrier, inc=1, device_id=peer, device_id_type=MESH)

    experts = lax.broadcasted_iota(jnp.int32, (n_slot, n_tok), 0)
    picks = [(routes[k : k + 1, :] == experts).astype(F32) for k in range(2)]
    row_id = lax.broadcasted_iota(jnp.int32, (n_tok, n_tok), 0)
    col_id = lax.broadcasted_iota(jnp.int32, (n_tok, n_tok), 1)
    before = (row_id < col_id).astype(BF16)
    earlier = dot((picks[0] + picks[1]).astype(BF16), before)
    same = lax.broadcasted_iota(jnp.int32, (n_slot, n_slot), 0) == lax.broadcasted_iota(jnp.int32, (n_slot, n_slot), 1)
    slot_of = jnp.sum(jnp.where(same, slots[...].astype(F32), 0.0), axis=1, keepdims=True)
    for k in range(2):
        pos = jnp.sum(picks[k] * earlier, axis=0, keepdims=True).astype(jnp.int32)
        dest = jnp.sum(picks[k] * slot_of, axis=0, keepdims=True).astype(jnp.int32)
        rel_z = (zh - ((dest >> 1) & (NR - 1)) + NR) & (NR - 1)
        rel_y = (y - (dest >> 3) + NR) & (NR - 1)
        place = (dest & 1) * ROWS + (rel_z * NR + rel_y) * PAIR + core * CAP + pos
        info[core, k : k + 1, :] = place.astype(F32)
        info[core, 2 + k : 3 + k, :] = combine[k : k + 1, :]

    pl.semaphore_wait(barrier, len(peers))
    loads[0].wait()
    send(TOK, tok.at[core], tok.at[core], sibling)
    send(INFO, info.at[core], info.at[core], sibling)
    for copy in loads[1:n_dense]:
        copy.wait()

    def w_slot(dz, dy, dc):
        return (dz * NR + dy) * 2 + dc

    hp = piece // 2

    def w_send(number, slot, target, device, half=None):
        if half is None:
            send(number, w_all.at[slot], w_all.at[target], device)
        else:
            rows = pl.ds(half * hp, hp)
            send(number, w_all.at[slot, :, rows, :], w_all.at[target, :, rows, :], device)

    def w_spread(dz):
        slot = w_slot(dz, 0, 0)
        w_send(WY + 4 * dz, slot, w_slot(dz, 3, 0), at_chip(1, 0))
        w_send(WY + 4 * dz + 1, slot, w_slot(dz, 1, 0), at_chip(-1, 0))

    def w_sibling(dz, dy):
        w_send(WS + dz * NR + dy, w_slot(dz, dy, 0), w_slot(dz, dy, 1), sibling)

    def w_across(dz, back):
        dy = 1 if back else 3
        arrived(WY + 4 * dz + back)
        w_send(WY + 4 * dz + 2 + back, w_slot(dz, dy, 0), w_slot(dz, 2, 0), at_chip(1 - 2 * back, 0), back)
        w_sibling(dz, dy)

    def w_last(dz):
        arrived(WY + 4 * dz + 2)
        arrived(WY + 4 * dz + 3)
        w_sibling(dz, 2)

    def w_start():
        w_send(WZ, w_slot(0, 0, 0), w_slot(3, 0, 0), at_chip(0, 1))
        w_send(WZ + 1, w_slot(0, 0, 0), w_slot(1, 0, 0), at_chip(0, -1))
        w_sibling(0, 0)

    def w_next(dz):
        arrived(WZ + (0 if dz == 3 else 1))
        w_spread(dz)
        w_sibling(dz, 0)

    def w_half(back):
        w_send(WZ + 2 + back, w_slot(1 if back else 3, 0, 0), w_slot(2, 0, 0), at_chip(0, 1 - 2 * back), back)

    def w_far():
        arrived(WZ + 2)
        arrived(WZ + 3)
        w_spread(2)
        w_sibling(2, 0)

    def w5():
        for number in range(NR * NR):
            arrived(WS + number)

    arrived(TOK)
    arrived(INFO)
    place = [
        jnp.concatenate([info[b, k : k + 1, :] for b in range(2)], axis=1).astype(jnp.int32) - core * ROWS
        for k in range(2)
    ]
    weight = [jnp.concatenate([info[b, 2 + k : 3 + k, :] for b in range(2)], axis=1) for k in range(2)]
    both = jnp.concatenate([tok[0], tok[1]], axis=0)
    zero_row = jnp.zeros((1, 2 * n_tok), F32)
    tables = []
    for k in range(2):
        high = weight[k].astype(BF16).astype(F32)
        rest = weight[k] - high
        middle = rest.astype(BF16).astype(F32)
        low = rest - middle
        first = zero_row + (1.0 - k)
        tables.append(jnp.concatenate([high, middle, low, first] + [zero_row] * 4, axis=0).astype(BF16))

    def pack(g):
        rows = lax.broadcasted_iota(jnp.int32, (CH, 2 * n_tok), 0) + g * CH
        picks = [(place[k] == rows).astype(F32) for k in range(2)]
        block = dot((picks[0] + picks[1]).astype(BF16), both).astype(BF16)
        marks = dot_nt(tables[0], picks[0].astype(BF16)) + dot_nt(tables[1], picks[1].astype(BF16))
        for dy in range(NR):
            n = g * NR + dy
            mark = marks[:, dy * PAIR : (dy + 1) * PAIR]
            if n == 0:
                x_all[0, 0:PAIR, :] = block[0:PAIR]
                meta_in[0, :, 0:PAIR] = mark
            else:
                meta_out[n, :, 0:PAIR] = mark
        if g == 0:
            outgoing[PAIR:CH, :] = block[PAIR:CH]
        else:
            outgoing[g * CH : (g + 1) * CH, :] = block

    def dispatch(g):
        for dy in range(NR):
            n = g * NR + dy
            if n:
                span = pl.ds(n * PAIR, PAIR)
                send(A2A + n, outgoing.at[span, :], x_all.at[0, span, :], at_chip(-dy, -g))
                send(META + n, meta_out.at[n], meta_in.at[n], at_chip(-dy, -g))

    def ag_send(g, number, slot, target, device, half=None):
        if half is None:
            rows = pl.ds(g * CH, CH)
        else:
            rows = pl.ds(g * CH + half * HALF, HALF)
        send(AG + 9 * g + number, x_all.at[slot, rows, :], x_all.at[target, rows, :], device)

    def ag_arrived(g, number):
        arrived(AG + 9 * g + number)

    def s1(g):
        for dy in range(NR):
            if g * NR + dy:
                arrived(A2A + g * NR + dy)
        ag_send(g, 0, 0, 4, partner)
        ag_send(g, 1, 0, 3, at_x(1))
        ag_send(g, 2, 0, 1, at_x(-1))

    def s2b(g):
        ag_arrived(g, 0)
        ag_send(g, 3, 4, 7, at_x(1))
        ag_send(g, 4, 4, 5, at_x(-1))

    def s2a(g, back):
        ag_arrived(g, 1 + back)
        ag_send(g, 5 + back, 1 if back else 3, 2, at_x(1 - 2 * back), back)

    def s3(g, back):
        ag_arrived(g, 3 + back)
        ag_send(g, 7 + back, 5 if back else 7, 6, at_x(1 - 2 * back), back)

    def dense_slots(t):
        found = []
        for j in range(4):
            e = t * 4 + j
            dz = ((e // 2) % NR - zh + NR) % NR
            dy = (e // (2 * NR) - y + NR) % NR
            dc = (j % 2 + core) % 2
            found.append(w_slot(dz, dy, dc))
        return found

    def features(g):
        parts = []
        for t in range(NZL * NR):
            slot = ((t // NR - zl + NZL) % NZL) * NR + (t % NR - x + NR) % NR
            parts.append(x_all[slot, pl.ds(g * CH, CH), :])
        return jnp.concatenate(parts, axis=1)

    def activate(gate, up, scale, g):
        spread = jnp.concatenate([scale[g * CH : (g + 1) * CH, :]] * (ff // 128), axis=1)
        return (silu(gate) * up * spread).astype(BF16)

    def s4(g):
        for number in range(5, 9):
            ag_arrived(g, number)
        rows = features(g)
        hidden[g, :, 0:ff] = activate(dot(rows, w_gate[...]), dot(rows, w_up[...]), scale_e, g)

    def dense(g):
        rows = features(g)
        order = [s for t in range(NZL * NR) for s in dense_slots(t)]
        gate = dot(rows, jnp.concatenate([w_all[s, 0] for s in order], axis=0))
        up = dot(rows, jnp.concatenate([w_all[s, 1] for s in order], axis=0))
        hidden[g, :, ff : 2 * ff] = activate(gate, up, scale_d, g)

    def scales():
        pick = lax.broadcasted_iota(jnp.int32, (PAIR, 128), 0) == lax.broadcasted_iota(jnp.int32, (PAIR, 128), 1)
        for n in range(NR * NR):
            if n:
                arrived(META + n)
            mark = meta_in[n]
            value = mark[0:1] + mark[1:2] + mark[2:3]
            first = mark[3:4]
            for row, target in ((value, scale_e), (first, scale_d)):
                column = jnp.sum(jnp.where(pick, row, 0.0), axis=1, keepdims=True)
                target[n * PAIR : (n + 1) * PAIR, :] = jnp.broadcast_to(column, (PAIR, 128))

    def down(g, dz, dx):
        t = ((zl + dz) % NZL) * NR + (x + dx) % NR
        cols = pl.ds(pl.multiple_of(t * width, width), width)
        blocks = []
        for s in dense_slots(t):
            block = w_all[s, 2]
            blocks.append(jnp.concatenate([block[:, 128 * j : 128 * (j + 1)] for j in range(ff // 128)], axis=0))
        weights = jnp.concatenate([w_down[:, cols], jnp.concatenate(blocks, axis=1)], axis=0)
        return dot(hidden[g], weights)

    def rs_number(g, number):
        return RS + 9 * g + number

    def rz(g):
        rs_send[g, 3] = down(g, 1, 2).astype(BF16)
        send(FAR + g, rs_send.at[g, 3], rs_far.at[g], partner)

    def r1(g, dz):
        part = down(g, dz, 2)
        if dz == 0 and g in BY_Z:
            arrived(FAR + g)
            part = part + rs_far[g].astype(F32)
        rs_send[g, 3 * dz] = part.astype(BF16)
        for back in range(2):
            rows = pl.ds(back * HALF, HALF)
            target = rs_half.at[g, 2 * dz + back]
            send(rs_number(g, 4 * dz + back), rs_send.at[g, 3 * dz, rows, :], target, at_x(1 - 2 * back))

    def r2(g, dz, back):
        part = down(g, dz, 3 if back else 1)
        slot = 3 * dz + 1 + back
        if dz == 1 and g in BY_Z:
            rs_send[g, slot] = part.astype(BF16)
        else:
            arrived(rs_number(g, 4 * dz + back))
            near, far = back * HALF, (1 - back) * HALF
            both_rows = part[near : near + HALF] + rs_half[g, 2 * dz + back].astype(F32)
            rs_send[g, slot, near : near + HALF, :] = both_rows.astype(BF16)
            rs_send[g, slot, far : far + HALF, :] = part[far : far + HALF].astype(BF16)
        target = rs_full.at[g, 2 * dz + back]
        send(rs_number(g, 4 * dz + 2 + back), rs_send.at[g, slot], target, at_x(1 - 2 * back))

    def gathered(g, dz):
        part = down(g, dz, 0)
        arrived(rs_number(g, 4 * dz + 2))
        arrived(rs_number(g, 4 * dz + 3))
        return part + rs_full[g, 2 * dz].astype(F32) + rs_full[g, 2 * dz + 1].astype(F32)

    def r3(g):
        rs_send[g, 6] = gathered(g, 1).astype(BF16)
        send(rs_number(g, 8), rs_send.at[g, 6], rs_z.at[g], partner)

    def r4(g):
        total = gathered(g, 0)
        arrived(rs_number(g, 8))
        total = (total + rs_z[g].astype(F32)).astype(BF16)
        if g == 0:
            returned[0:PAIR, :] = total[0:PAIR]
            result[PAIR:CH, :] = total[PAIR:CH]
        else:
            result[g * CH : (g + 1) * CH, :] = total
        for dy in range(NR):
            n = g * NR + dy
            if n:
                span = pl.ds(n * PAIR, PAIR)
                send(RET + n, result.at[span, :], returned.at[span, :], at_chip(dy, g))

    eye = (col_id == row_id).astype(F32)

    def column(b, k):
        row = info[b, k : k + 1, :]
        return jnp.sum(eye * row, axis=1, keepdims=True).astype(jnp.int32) - core * ROWS

    own_cols = [column(core, k) for k in range(2)]
    other_cols = [column(1 - core, k) for k in range(2)]
    part_send[...] = jnp.zeros_like(part_send)
    part_own[...] = tok[core].astype(F32)

    def combine_rows(g):
        for dy in range(NR):
            if g * NR + dy:
                arrived(RET + g * NR + dy)
        rows = lax.broadcasted_iota(jnp.int32, (n_tok, CH), 1) + g * CH
        block = returned[g * CH : (g + 1) * CH, :]
        for cols, target in ((other_cols, part_send), (own_cols, part_own)):
            chosen = (cols[0] == rows).astype(F32) + (cols[1] == rows).astype(F32)
            target[...] += dot(chosen.astype(BF16), block)

    def exchange():
        send(SIB, part_send, part_recv, sibling)
        arrived(SIB)
        out[...] = (part_own[...] + part_recv[...]).astype(BF16)

    w_start()
    w_spread(0)
    pack(0)
    pack(1)
    pack(3)
    dispatch(0)
    dispatch(1)
    w_across(0, 0)
    s1(0)
    dispatch(3)
    s1(1)
    s2a(0, 1)
    w_next(3)
    s2a(0, 0)
    s1(3)
    s2a(1, 1)
    s2a(1, 0)
    w_across(3, 0)
    w_next(1)
    s2b(0)
    w_half(0)
    w_half(1)
    w_across(0, 1)
    w_across(1, 1)
    s2b(1)
    s3(0, 1)
    w_across(3, 1)
    pack(2)
    s2a(3, 1)
    dispatch(2)
    s3(0, 0)
    w_across(1, 0)
    scales()
    s2b(3)
    s3(1, 0)
    w_far()
    for copy in loads[n_dense:]:
        copy.wait()
    s4(0)
    s2a(3, 0)
    s3(1, 1)
    s3(3, 0)
    s3(3, 1)
    w_last(3)
    w_last(1)
    w_last(0)
    s1(2)
    w_across(2, 0)
    w_across(2, 1)
    s4(1)
    w_last(2)
    s2b(2)
    w5()
    dense(1)
    s2a(2, 0)
    s2a(2, 1)
    rz(1)
    s3(2, 0)
    s3(2, 1)
    dense(0)
    r1(0, 1)
    r2(1, 1, 1)
    r2(1, 1, 0)
    s4(2)
    dense(2)
    r2(2, 1, 0)
    r2(2, 1, 1)
    rz(2)
    r2(0, 1, 0)
    r2(0, 1, 1)
    s4(3)
    r3(1)
    r1(2, 0)
    dense(3)
    rz(3)
    r2(3, 1, 0)
    r2(3, 1, 1)
    r3(2)
    r2(2, 0, 1)
    r2(2, 0, 0)
    r1(1, 0)
    r3(0)
    r1(3, 0)
    r3(3)
    r2(1, 0, 0)
    r2(1, 0, 1)
    r4(2)
    r2(3, 0, 0)
    r1(0, 0)
    r2(3, 0, 1)
    r2(0, 0, 0)
    r4(1)
    r2(0, 0, 1)
    r4(3)
    combine_rows(2)
    r4(0)
    combine_rows(1)
    combine_rows(0)
    combine_rows(3)
    exchange()

    for copy in sent.values():
        copy.wait_send()


def body(tokens, routes, combine, expert_slot, dense_gate, dense_up, dense_down, expert_gate, expert_up, expert_down):
    n_tok, width = tokens.shape
    depth, ff = expert_gate.shape[1:]
    piece = dense_gate.shape[0]
    any_spec = pl.BlockSpec(memory_space=pl.ANY)
    vmem = pl.BlockSpec(memory_space=pltpu.VMEM)
    n_slots = NZL * NR
    return pl.pallas_call(
        kernel,
        out_shape=jax.ShapeDtypeStruct((n_tok, width), BF16),
        in_specs=[any_spec, vmem, vmem, vmem] + [any_spec] * 6,
        out_specs=vmem,
        scratch_shapes=[
            pltpu.VMEM((2, n_tok, width), BF16),
            pltpu.VMEM((2, 8, n_tok), F32),
            pltpu.VMEM((NR * NR, 8, 128), F32),
            pltpu.VMEM((NR * NR, 8, 128), F32),
            pltpu.VMEM((ROWS, 128), F32),
            pltpu.VMEM((ROWS, 128), F32),
            pltpu.VMEM((depth, ff), BF16),
            pltpu.VMEM((depth, ff), BF16),
            pltpu.VMEM((ff, depth), BF16),
            pltpu.VMEM((2 * NR * NR, 3, piece, ff), BF16),
            pltpu.VMEM((ROWS, width), BF16),
            pltpu.VMEM((n_slots, ROWS, width), BF16),
            pltpu.VMEM((NR, CH, 2 * ff), BF16),
            pltpu.VMEM((NR, 7, CH, width), BF16),
            pltpu.VMEM((NR, 4, HALF, width), BF16),
            pltpu.VMEM((NR, 4, CH, width), BF16),
            pltpu.VMEM((NR, CH, width), BF16),
            pltpu.VMEM((NR, CH, width), BF16),
            pltpu.VMEM((ROWS, width), BF16),
            pltpu.VMEM((ROWS, width), BF16),
            pltpu.VMEM((n_tok, width), F32),
            pltpu.VMEM((n_tok, width), F32),
            pltpu.VMEM((n_tok, width), F32),
            pltpu.SemaphoreType.DMA((N_SEM,)),
            pltpu.SemaphoreType.DMA((N_SEM,)),
            pltpu.SemaphoreType.DMA((9,)),
        ],
        compiler_params=pltpu.CompilerParams(
            collective_id=0, has_side_effects=True, vmem_limit_bytes=60 * 1024 * 1024
        ),
    )(
        tokens,
        routes.T,
        combine.T,
        expert_slot.reshape(1, -1),
        dense_gate,
        dense_up,
        dense_down,
        expert_gate,
        expert_up,
        expert_down,
    )


def solution(mesh):
    in_specs = (
        P("ep", "tp"),
        P("ep", None),
        P("ep", None),
        P(),
        P("ep", "tp"),
        P("ep", "tp"),
        P("tp", "ep"),
        P("ep", None, "tp"),
        P("ep", None, "tp"),
        P("ep", "tp", None),
    )
    out_specs = P("ep", "tp")
    return jax.shard_map(body, mesh=mesh, in_specs=in_specs, out_specs=out_specs, check_vma=False)
```

```python
import jax
import jax.numpy as jnp
from jax import lax
from jax.experimental import pallas as pl
from jax.experimental.pallas import tpu as pltpu
from jax.sharding import PartitionSpec as P

MESH = pl.DeviceIdType.MESH
BF16 = jnp.bfloat16
F32 = jnp.float32

NR = 4
NZL = 2
CAP = 24
PAIR = 2 * CAP
ROWS = NR * NR * PAIR
CH = NR * PAIR
HALF = CH // 2
BY_Z = (0, 1, 2, 3)
N_SEM = 164

A2A, META, TOK, INFO, AG, WZ, WY, WS, RS, RET, SIB, FAR = 0, 16, 32, 33, 34, 70, 74, 90, 106, 142, 158, 160


def dot(a, b):
    return jnp.dot(a, b, preferred_element_type=F32)


def dot_nt(a, b):
    return lax.dot_general(a, b, (((1,), (1,)), ((), ())), preferred_element_type=F32)


def silu(v):
    return v / (1.0 + jnp.exp(-v))


def kernel(
    tokens,
    routes,
    combine,
    slots,
    dense_gate,
    dense_up,
    dense_down,
    expert_gate,
    expert_up,
    expert_down,
    out,
    tok,
    info,
    meta_out,
    meta_in,
    scale_e,
    scale_d,
    w_gate,
    w_up,
    w_down,
    w_all,
    outgoing,
    x_all,
    hidden,
    rs_send,
    rs_half,
    rs_full,
    rs_z,
    rs_far,
    result,
    returned,
    part_send,
    part_recv,
    part_own,
    send_sem,
    recv_sem,
    load_sem,
):
    n_tok, width = tokens.shape
    n_slot = slots.shape[1]
    ff = w_gate.shape[1]
    piece = dense_gate.shape[0]
    tp = lax.axis_index("tp")
    ep = lax.axis_index("ep")
    x, zl = tp % NR, tp // NR
    core, zh, y = ep % 2, (ep // 2) % NR, ep // (2 * NR)

    def at_x(d):
        return {"tp": zl * NR + (x + d + NR) % NR, "ep": ep}

    def at_chip(dy, dz):
        return {"tp": tp, "ep": ((y + dy + NR) % NR) * (2 * NR) + ((zh + dz + NR) % NR) * 2 + core}

    partner = {"tp": (1 - zl) * NR + x, "ep": ep}
    sibling = {"tp": tp, "ep": ep + 1 - 2 * core}

    sent = {}

    def send(number, src, dst, device):
        copy = pltpu.make_async_remote_copy(
            src_ref=src,
            dst_ref=dst,
            send_sem=send_sem.at[number],
            recv_sem=recv_sem.at[number],
            device_id=device,
            device_id_type=MESH,
        )
        copy.start()
        sent[number] = copy

    def arrived(number):
        sent[number].wait_recv()

    loads = []

    def load(src, dst):
        copy = pltpu.make_async_copy(src, dst, load_sem.at[len(loads)])
        copy.start()
        loads.append(copy)

    load(tokens, tok.at[core])
    load(dense_gate, w_all.at[0, 0])
    load(dense_up, w_all.at[0, 1])
    for j in range(ff // 128):
        load(dense_down.at[pl.ds(128 * j, 128), :], w_all.at[0, 2, :, pl.ds(128 * j, 128)])
    n_dense = len(loads)
    load(expert_gate.at[0], w_gate)
    load(expert_up.at[0], w_up)
    load(expert_down.at[0], w_down)

    peers = [partner, sibling, at_x(1), at_x(-1)]
    peers += [at_chip(dy, dz) for dz in range(NR) for dy in range(NR) if dy or dz]
    barrier = pltpu.get_barrier_semaphore()
    for peer in peers:
        pl.semaphore_signal(barrier, inc=1, device_id=peer, device_id_type=MESH)

    experts = lax.broadcasted_iota(jnp.int32, (n_slot, n_tok), 0)
    picks = [(routes[k : k + 1, :] == experts).astype(F32) for k in range(2)]
    row_id = lax.broadcasted_iota(jnp.int32, (n_tok, n_tok), 0)
    col_id = lax.broadcasted_iota(jnp.int32, (n_tok, n_tok), 1)
    before = (row_id < col_id).astype(BF16)
    earlier = dot((picks[0] + picks[1]).astype(BF16), before)
    same = lax.broadcasted_iota(jnp.int32, (n_slot, n_slot), 0) == lax.broadcasted_iota(jnp.int32, (n_slot, n_slot), 1)
    slot_of = jnp.sum(jnp.where(same, slots[...].astype(F32), 0.0), axis=1, keepdims=True)
    for k in range(2):
        pos = jnp.sum(picks[k] * earlier, axis=0, keepdims=True).astype(jnp.int32)
        dest = jnp.sum(picks[k] * slot_of, axis=0, keepdims=True).astype(jnp.int32)
        rel_z = (zh - ((dest >> 1) & (NR - 1)) + NR) & (NR - 1)
        rel_y = (y - (dest >> 3) + NR) & (NR - 1)
        place = (dest & 1) * ROWS + (rel_z * NR + rel_y) * PAIR + core * CAP + pos
        info[core, k : k + 1, :] = place.astype(F32)
        info[core, 2 + k : 3 + k, :] = combine[k : k + 1, :]

    pl.semaphore_wait(barrier, len(peers))
    loads[0].wait()
    send(TOK, tok.at[core], tok.at[core], sibling)
    send(INFO, info.at[core], info.at[core], sibling)
    for copy in loads[1:n_dense]:
        copy.wait()

    def w_slot(dz, dy, dc):
        return (dz * NR + dy) * 2 + dc

    hp = piece // 2

    def w_send(number, slot, target, device, half=None):
        if half is None:
            send(number, w_all.at[slot], w_all.at[target], device)
        else:
            rows = pl.ds(half * hp, hp)
            send(number, w_all.at[slot, :, rows, :], w_all.at[target, :, rows, :], device)

    def w_spread(dz):
        slot = w_slot(dz, 0, 0)
        w_send(WY + 4 * dz, slot, w_slot(dz, 3, 0), at_chip(1, 0))
        w_send(WY + 4 * dz + 1, slot, w_slot(dz, 1, 0), at_chip(-1, 0))

    def w_sibling(dz, dy):
        w_send(WS + dz * NR + dy, w_slot(dz, dy, 0), w_slot(dz, dy, 1), sibling)

    def w_across(dz, back):
        dy = 1 if back else 3
        arrived(WY + 4 * dz + back)
        w_send(WY + 4 * dz + 2 + back, w_slot(dz, dy, 0), w_slot(dz, 2, 0), at_chip(1 - 2 * back, 0), back)
        w_sibling(dz, dy)

    def w_last(dz):
        arrived(WY + 4 * dz + 2)
        arrived(WY + 4 * dz + 3)
        w_sibling(dz, 2)

    def w_start():
        w_send(WZ, w_slot(0, 0, 0), w_slot(3, 0, 0), at_chip(0, 1))
        w_send(WZ + 1, w_slot(0, 0, 0), w_slot(1, 0, 0), at_chip(0, -1))
        w_sibling(0, 0)

    def w_next(dz):
        arrived(WZ + (0 if dz == 3 else 1))
        w_spread(dz)
        w_sibling(dz, 0)

    def w_half(back):
        w_send(WZ + 2 + back, w_slot(1 if back else 3, 0, 0), w_slot(2, 0, 0), at_chip(0, 1 - 2 * back), back)

    def w_far():
        arrived(WZ + 2)
        arrived(WZ + 3)
        w_spread(2)
        w_sibling(2, 0)

    def w5():
        for number in range(NR * NR):
            arrived(WS + number)

    arrived(TOK)
    arrived(INFO)
    place = [
        jnp.concatenate([info[b, k : k + 1, :] for b in range(2)], axis=1).astype(jnp.int32) - core * ROWS
        for k in range(2)
    ]
    weight = [jnp.concatenate([info[b, 2 + k : 3 + k, :] for b in range(2)], axis=1) for k in range(2)]
    both = jnp.concatenate([tok[0], tok[1]], axis=0)
    zero_row = jnp.zeros((1, 2 * n_tok), F32)
    tables = []
    for k in range(2):
        high = weight[k].astype(BF16).astype(F32)
        rest = weight[k] - high
        middle = rest.astype(BF16).astype(F32)
        low = rest - middle
        first = zero_row + (1.0 - k)
        tables.append(jnp.concatenate([high, middle, low, first] + [zero_row] * 4, axis=0).astype(BF16))

    def pack(g):
        rows = lax.broadcasted_iota(jnp.int32, (CH, 2 * n_tok), 0) + g * CH
        picks = [(place[k] == rows).astype(F32) for k in range(2)]
        block = dot((picks[0] + picks[1]).astype(BF16), both).astype(BF16)
        marks = dot_nt(tables[0], picks[0].astype(BF16)) + dot_nt(tables[1], picks[1].astype(BF16))
        for dy in range(NR):
            n = g * NR + dy
            mark = marks[:, dy * PAIR : (dy + 1) * PAIR]
            if n == 0:
                x_all[0, 0:PAIR, :] = block[0:PAIR]
                meta_in[0, :, 0:PAIR] = mark
            else:
                meta_out[n, :, 0:PAIR] = mark
        if g == 0:
            outgoing[PAIR:CH, :] = block[PAIR:CH]
        else:
            outgoing[g * CH : (g + 1) * CH, :] = block

    def dispatch(g):
        for dy in range(NR):
            n = g * NR + dy
            if n:
                span = pl.ds(n * PAIR, PAIR)
                send(A2A + n, outgoing.at[span, :], x_all.at[0, span, :], at_chip(-dy, -g))
                send(META + n, meta_out.at[n], meta_in.at[n], at_chip(-dy, -g))

    def ag_send(g, number, slot, target, device, half=None):
        if half is None:
            rows = pl.ds(g * CH, CH)
        else:
            rows = pl.ds(g * CH + half * HALF, HALF)
        send(AG + 9 * g + number, x_all.at[slot, rows, :], x_all.at[target, rows, :], device)

    def ag_arrived(g, number):
        arrived(AG + 9 * g + number)

    def s1(g):
        for dy in range(NR):
            if g * NR + dy:
                arrived(A2A + g * NR + dy)
        ag_send(g, 0, 0, 4, partner)
        ag_send(g, 1, 0, 3, at_x(1))
        ag_send(g, 2, 0, 1, at_x(-1))

    def s2b(g):
        ag_arrived(g, 0)
        ag_send(g, 3, 4, 7, at_x(1))
        ag_send(g, 4, 4, 5, at_x(-1))

    def s2a(g, back):
        ag_arrived(g, 1 + back)
        ag_send(g, 5 + back, 1 if back else 3, 2, at_x(1 - 2 * back), back)

    def s3(g, back):
        ag_arrived(g, 3 + back)
        ag_send(g, 7 + back, 5 if back else 7, 6, at_x(1 - 2 * back), back)

    def dense_slots(t):
        found = []
        for j in range(4):
            e = t * 4 + j
            dz = ((e // 2) % NR - zh + NR) % NR
            dy = (e // (2 * NR) - y + NR) % NR
            dc = (j % 2 + core) % 2
            found.append(w_slot(dz, dy, dc))
        return found

    def features(g):
        parts = []
        for t in range(NZL * NR):
            slot = ((t // NR - zl + NZL) % NZL) * NR + (t % NR - x + NR) % NR
            parts.append(x_all[slot, pl.ds(g * CH, CH), :])
        return jnp.concatenate(parts, axis=1)

    def activate(gate, up, scale, g):
        spread = jnp.concatenate([scale[g * CH : (g + 1) * CH, :]] * (ff // 128), axis=1)
        return (silu(gate) * up * spread).astype(BF16)

    def s4(g):
        for number in range(5, 9):
            ag_arrived(g, number)
        rows = features(g)
        hidden[g, :, 0:ff] = activate(dot(rows, w_gate[...]), dot(rows, w_up[...]), scale_e, g)

    def dense(g):
        rows = features(g)
        order = [s for t in range(NZL * NR) for s in dense_slots(t)]
        gate = dot(rows, jnp.concatenate([w_all[s, 0] for s in order], axis=0))
        up = dot(rows, jnp.concatenate([w_all[s, 1] for s in order], axis=0))
        hidden[g, :, ff : 2 * ff] = activate(gate, up, scale_d, g)

    def scales():
        pick = lax.broadcasted_iota(jnp.int32, (PAIR, 128), 0) == lax.broadcasted_iota(jnp.int32, (PAIR, 128), 1)
        for n in range(NR * NR):
            if n:
                arrived(META + n)
            mark = meta_in[n]
            value = mark[0:1] + mark[1:2] + mark[2:3]
            first = mark[3:4]
            for row, target in ((value, scale_e), (first, scale_d)):
                column = jnp.sum(jnp.where(pick, row, 0.0), axis=1, keepdims=True)
                target[n * PAIR : (n + 1) * PAIR, :] = jnp.broadcast_to(column, (PAIR, 128))

    def down(g, dz, dx):
        t = ((zl + dz) % NZL) * NR + (x + dx) % NR
        cols = pl.ds(pl.multiple_of(t * width, width), width)
        blocks = []
        for s in dense_slots(t):
            block = w_all[s, 2]
            blocks.append(jnp.concatenate([block[:, 128 * j : 128 * (j + 1)] for j in range(ff // 128)], axis=0))
        weights = jnp.concatenate([w_down[:, cols], jnp.concatenate(blocks, axis=1)], axis=0)
        return dot(hidden[g], weights)

    def rs_number(g, number):
        return RS + 9 * g + number

    def rz(g):
        rs_send[g, 3] = down(g, 1, 2).astype(BF16)
        send(FAR + g, rs_send.at[g, 3], rs_far.at[g], partner)

    def r1(g, dz):
        part = down(g, dz, 2)
        if dz == 0 and g in BY_Z:
            arrived(FAR + g)
            part = part + rs_far[g].astype(F32)
        rs_send[g, 3 * dz] = part.astype(BF16)
        for back in range(2):
            rows = pl.ds(back * HALF, HALF)
            target = rs_half.at[g, 2 * dz + back]
            send(rs_number(g, 4 * dz + back), rs_send.at[g, 3 * dz, rows, :], target, at_x(1 - 2 * back))

    def r2(g, dz, back):
        part = down(g, dz, 3 if back else 1)
        slot = 3 * dz + 1 + back
        if dz == 1 and g in BY_Z:
            rs_send[g, slot] = part.astype(BF16)
        else:
            arrived(rs_number(g, 4 * dz + back))
            near, far = back * HALF, (1 - back) * HALF
            both_rows = part[near : near + HALF] + rs_half[g, 2 * dz + back].astype(F32)
            rs_send[g, slot, near : near + HALF, :] = both_rows.astype(BF16)
            rs_send[g, slot, far : far + HALF, :] = part[far : far + HALF].astype(BF16)
        target = rs_full.at[g, 2 * dz + back]
        send(rs_number(g, 4 * dz + 2 + back), rs_send.at[g, slot], target, at_x(1 - 2 * back))

    def gathered(g, dz):
        part = down(g, dz, 0)
        arrived(rs_number(g, 4 * dz + 2))
        arrived(rs_number(g, 4 * dz + 3))
        return part + rs_full[g, 2 * dz].astype(F32) + rs_full[g, 2 * dz + 1].astype(F32)

    def r3(g):
        rs_send[g, 6] = gathered(g, 1).astype(BF16)
        send(rs_number(g, 8), rs_send.at[g, 6], rs_z.at[g], partner)

    def r4(g):
        total = gathered(g, 0)
        arrived(rs_number(g, 8))
        total = (total + rs_z[g].astype(F32)).astype(BF16)
        if g == 0:
            returned[0:PAIR, :] = total[0:PAIR]
            result[PAIR:CH, :] = total[PAIR:CH]
        else:
            result[g * CH : (g + 1) * CH, :] = total
        for dy in range(NR):
            n = g * NR + dy
            if n:
                span = pl.ds(n * PAIR, PAIR)
                send(RET + n, result.at[span, :], returned.at[span, :], at_chip(dy, g))

    eye = (col_id == row_id).astype(F32)

    def column(b, k):
        row = info[b, k : k + 1, :]
        return jnp.sum(eye * row, axis=1, keepdims=True).astype(jnp.int32) - core * ROWS

    own_cols = [column(core, k) for k in range(2)]
    other_cols = [column(1 - core, k) for k in range(2)]
    part_send[...] = jnp.zeros_like(part_send)
    part_own[...] = tok[core].astype(F32)

    def combine_rows(g):
        for dy in range(NR):
            if g * NR + dy:
                arrived(RET + g * NR + dy)
        rows = lax.broadcasted_iota(jnp.int32, (n_tok, CH), 1) + g * CH
        block = returned[g * CH : (g + 1) * CH, :]
        for cols, target in ((other_cols, part_send), (own_cols, part_own)):
            chosen = (cols[0] == rows).astype(F32) + (cols[1] == rows).astype(F32)
            target[...] += dot(chosen.astype(BF16), block)

    def exchange():
        send(SIB, part_send, part_recv, sibling)
        arrived(SIB)
        out[...] = (part_own[...] + part_recv[...]).astype(BF16)

    w_start()
    w_spread(0)
    pack(1)
    pack(3)
    pack(2)
    pack(0)
    dispatch(3)
    dispatch(0)
    s1(0)
    w_across(0, 1)
    dispatch(1)
    s2a(0, 1)
    s2a(0, 0)
    s1(3)
    w_next(1)
    s2a(3, 0)
    s2a(3, 1)
    w_next(3)
    w_across(0, 0)
    s1(1)
    s2b(0)
    w_across(1, 1)
    w_half(0)
    w_half(1)
    w_across(3, 1)
    s2b(3)
    w_across(3, 0)
    s3(0, 0)
    s2b(1)
    w_across(1, 0)
    s3(0, 1)
    w_last(0)
    dispatch(2)
    scales()
    w_far()
    w_last(3)
    s3(3, 1)
    s3(3, 0)
    for copy in loads[n_dense:]:
        copy.wait()
    s4(0)
    s3(1, 0)
    s2a(1, 1)
    s3(1, 1)
    s2a(1, 0)
    s4(3)
    s1(2)
    w_last(1)
    w_across(2, 1)
    w_across(2, 0)
    s4(1)
    s2b(2)
    w_last(2)
    w5()
    dense(3)
    r2(3, 1, 1)
    s2a(2, 1)
    rz(3)
    s2a(2, 0)
    dense(1)
    s3(2, 0)
    s3(2, 1)
    dense(0)
    rz(1)
    r2(3, 1, 0)
    r2(0, 1, 0)
    rz(0)
    r1(3, 0)
    r2(0, 1, 1)
    s4(2)
    dense(2)
    rz(2)
    r2(2, 1, 1)
    r2(2, 1, 0)
    r3(0)
    r1(1, 0)
    r1(2, 0)
    r3(3)
    r2(1, 1, 0)
    r2(1, 1, 1)
    r3(2)
    r2(2, 0, 1)
    r2(2, 0, 0)
    r3(1)
    r2(3, 0, 1)
    r2(3, 0, 0)
    r4(2)
    r2(1, 0, 1)
    r1(0, 0)
    r2(1, 0, 0)
    r2(0, 0, 1)
    r2(0, 0, 0)
    r4(3)
    r4(1)
    r4(0)
    combine_rows(2)
    combine_rows(3)
    combine_rows(0)
    combine_rows(1)
    exchange()

    for copy in sent.values():
        copy.wait_send()


def body(tokens, routes, combine, expert_slot, dense_gate, dense_up, dense_down, expert_gate, expert_up, expert_down):
    n_tok, width = tokens.shape
    depth, ff = expert_gate.shape[1:]
    piece = dense_gate.shape[0]
    any_spec = pl.BlockSpec(memory_space=pl.ANY)
    vmem = pl.BlockSpec(memory_space=pltpu.VMEM)
    n_slots = NZL * NR
    return pl.pallas_call(
        kernel,
        out_shape=jax.ShapeDtypeStruct((n_tok, width), BF16),
        in_specs=[any_spec, vmem, vmem, vmem] + [any_spec] * 6,
        out_specs=vmem,
        scratch_shapes=[
            pltpu.VMEM((2, n_tok, width), BF16),
            pltpu.VMEM((2, 8, n_tok), F32),
            pltpu.VMEM((NR * NR, 8, 128), F32),
            pltpu.VMEM((NR * NR, 8, 128), F32),
            pltpu.VMEM((ROWS, 128), F32),
            pltpu.VMEM((ROWS, 128), F32),
            pltpu.VMEM((depth, ff), BF16),
            pltpu.VMEM((depth, ff), BF16),
            pltpu.VMEM((ff, depth), BF16),
            pltpu.VMEM((2 * NR * NR, 3, piece, ff), BF16),
            pltpu.VMEM((ROWS, width), BF16),
            pltpu.VMEM((n_slots, ROWS, width), BF16),
            pltpu.VMEM((NR, CH, 2 * ff), BF16),
            pltpu.VMEM((NR, 7, CH, width), BF16),
            pltpu.VMEM((NR, 4, HALF, width), BF16),
            pltpu.VMEM((NR, 4, CH, width), BF16),
            pltpu.VMEM((NR, CH, width), BF16),
            pltpu.VMEM((NR, CH, width), BF16),
            pltpu.VMEM((ROWS, width), BF16),
            pltpu.VMEM((ROWS, width), BF16),
            pltpu.VMEM((n_tok, width), F32),
            pltpu.VMEM((n_tok, width), F32),
            pltpu.VMEM((n_tok, width), F32),
            pltpu.SemaphoreType.DMA((N_SEM,)),
            pltpu.SemaphoreType.DMA((N_SEM,)),
            pltpu.SemaphoreType.DMA((9,)),
        ],
        compiler_params=pltpu.CompilerParams(
            collective_id=0, has_side_effects=True, vmem_limit_bytes=60 * 1024 * 1024
        ),
    )(
        tokens,
        routes.T,
        combine.T,
        expert_slot.reshape(1, -1),
        dense_gate,
        dense_up,
        dense_down,
        expert_gate,
        expert_up,
        expert_down,
    )


def solution(mesh):
    in_specs = (
        P("ep", "tp"),
        P("ep", None),
        P("ep", None),
        P(),
        P("ep", "tp"),
        P("ep", "tp"),
        P("tp", "ep"),
        P("ep", None, "tp"),
        P("ep", None, "tp"),
        P("ep", "tp", None),
    )
    out_specs = P("ep", "tp")
    return jax.shard_map(body, mesh=mesh, in_specs=in_specs, out_specs=out_specs, check_vma=False)
```
